32 devices in a mesh: groups: 2 (over x), rows: 8 (over z, y), cols: 2 (over core).
Axes of the slice: x: 2, y: 2, z: 4, core: 2. Of those that a mesh axis runs over, the one named last changes fastest.
Arguments:
- features: bfloat16 [80, 256, 1024], P(('groups', 'rows'), 'cols'), parts along dimension 0, may hold values from -6 to 6
- upstream: bfloat16 [80, 256, 1024], P(('groups', 'rows'), 'cols'), parts along dimension 0, may hold values from -6 to 6
- tile_valid: int32 [10, 32], P('groups'), parts along dimension 0, may hold values 0 or 1
- depthwise: bfloat16 [7, 7, 1024], replicated, may hold values from -0.875 to 0.875
- depthbias: float32 [1024], replicated, may hold values from -4 to 4
- norm_gain: float32 [1024], replicated, may hold values from 0.1 to 1.9
- norm_shift: float32 [1024], replicated, may hold values from -3 to 3
- expand: bfloat16 [1024, 2048], replicated, may hold values from -0.1875 to 0.1875
- expandbias: float32 [2048], replicated, may hold values from -3 to 3
- project: bfloat16 [2048, 1024], replicated, may hold values from -0.125 to 0.125
- projectbias: float32 [1024], replicated, may hold values from -4 to 4
- layer_scale: float32 [1024], replicated, may hold values from -4 to 4
Outputs:
- features_grad: bfloat16 [80, 256, 1024], P(('groups', 'rows'), 'cols'), parts along dimension 0
- depthwise_grad: float32 [14, 7, 1024], P('groups'), parts along dimension 0
- depthbias_grad: float32 [2048], P('groups'), parts along dimension 0
- gain_grad: float32 [2048], P('groups'), parts along dimension 0
- shift_grad: float32 [2048], P('groups'), parts along dimension 0
- expand_grad: float32 [2048, 2048], P(('groups', 'rows', 'cols')), parts along dimension 0
- expandbias_grad: float32 [4096], P('groups'), parts along dimension 0
- project_grad: float32 [4096, 1024], P(('groups', 'rows', 'cols')), parts along dimension 0
- projectbias_grad: float32 [2048], P('groups'), parts along dimension 0
- scale_grad: float32 [2048], P('groups'), parts along dimension 0
The draws below stay inside these ranges and needn't reach their ends.
There are 2 independent parts, one for each index of `groups`. The reference program is written for one: setup_inputs(seed, part) draws one part's arguments, and reference() takes and returns one part's arrays. A program takes and returns all parts, laid end to end along the dimension named above; an argument that names none is the same for every part. Nothing has to cross between parts.
Inputs may be any that keep to these rules, and one draw needn't show every extreme that they name: `tile_valid`: 1 marks a tile of 8 x 8 cells with data.
All inputs are finite; a program needn't handle non-finite values.
Results may differ from the reference program's by a relative error of at most 0.0063.
Values may be sent and summed in bfloat16 or wider, within the bound.
A program may use at most 128 MiB of HBM per device.

```python
import jax
import jax.numpy as jnp
from jax import lax

C = 1024
F = 2048
NH = 40
NW = 256
TR = 5
TC = 32


def touch_ends(drawn, rng, least, largest):
    extent = drawn.shape
    index_at = [jax.random.randint(jax.random.fold_in(rng, axis), (), 0, extent[axis]) for axis in range(len(extent))]
    drawn = drawn.at[tuple(index_at)].set(least)
    longest = extent.index(max(extent))
    index_at[longest] = (index_at[longest] + 1) % extent[longest]
    return drawn.at[tuple(index_at)].set(largest)


def levels(rng, dims, shards, least, top_value):
    def one(position, parts):
        heights = jax.random.uniform(jax.random.fold_in(jax.random.fold_in(rng, 6), position), (parts,), jnp.float32, least / len(shards), top_value / len(shards))
        return jnp.repeat(jnp.exp(heights), dims[position] // parts).reshape((-1,) + (1,) * (len(dims) - position - 1))

    factor_of = one(*shards[0])
    for cut in shards[1:]:
        factor_of = factor_of * one(*cut)
    return factor_of


def noise(stream_key, extent, deviation, limit, split=(), dtype=jnp.bfloat16):
    values = jax.random.normal(stream_key, extent, jnp.float32) * deviation
    if len(split) > 0:
        values = levels(stream_key, extent, split, -0.22, 0.18) * values
    return jnp.clip(values, min=-limit, max=limit).astype(dtype)


def setup_inputs(seed: int = 0, part: int = 0) -> dict:
    arg_keys = jax.random.split(jax.random.key(seed), 13)
    part_splits = jax.random.split(jax.random.fold_in(arg_keys[12], part), 13)
    return {
        "features": noise(part_splits[0], (NH, NW, C), 1.0, 6.0, ((0, 8), (1, 2))),
        "upstream": noise(part_splits[1], (NH, NW, C), 1.0, 6.0, ((0, 8), (1, 2))),
        "tile_valid": touch_ends((jax.random.randint(part_splits[2], (TR, TC), 0, 4) < 3).astype(jnp.int32), jax.random.fold_in(part_splits[2], 1), 0, 1),
        "depthwise": noise(arg_keys[3], (7, 7, C), 49 ** -0.5, 0.875),
        "depthbias": noise(arg_keys[4], (C,), 1.0, 4.0, (), jnp.float32),
        "norm_gain": jnp.clip(1.0 + 0.18 * jax.random.normal(arg_keys[5], (C,), jnp.float32), 0.1, 1.9),
        "norm_shift": noise(arg_keys[6], (C,), 0.5, 3.0, (), jnp.float32),
        "expand": noise(arg_keys[7], (C, F), C ** -0.5, 0.1875),
        "expandbias": noise(arg_keys[8], (F,), 0.5, 3.0, (), jnp.float32),
        "project": noise(arg_keys[9], (F, C), F ** -0.5, 0.125),
        "projectbias": noise(arg_keys[10], (C,), 1.0, 4.0, (), jnp.float32),
        "layer_scale": noise(arg_keys[11], (C,), 1.0, 4.0, (), jnp.float32),
    }


def depth_conv(padded, depthwise, height, breadth):
    total = jnp.zeros((height, breadth, padded.shape[2]), jnp.float32)
    for row_off in range(7):
        for col_off in range(7):
            window = padded[row_off:row_off + height, col_off:col_off + breadth].astype(jnp.float32)
            total = total + window * depthwise[row_off, col_off].astype(jnp.float32)
    return total

def kernel_sums(padded, grad_cells, height, breadth):
    rows_out = []
    for row_off in range(7):
        for col_off in range(7):
            window = padded[row_off:row_off + height, col_off:col_off + breadth].astype(jnp.float32)
            rows_out.append(lax.optimization_barrier(jnp.sum(window * grad_cells, axis=(0, 1))))
    return jnp.stack(rows_out).reshape(7, 7, grad_cells.shape[2])

def reference(features, upstream, tile_valid, depthwise, depthbias, norm_gain, norm_shift, expand, expandbias, project, projectbias, layer_scale):
    height, breadth, width = features.shape
    padded = jnp.pad(features, ((3, 3), (3, 3), (0, 0)))
    mixed = depth_conv(padded, depthwise, height, breadth) + depthbias
    centred = mixed - lax.optimization_barrier(jnp.mean(mixed, axis=-1, keepdims=True))
    rstd = lax.rsqrt(lax.optimization_barrier(jnp.mean(centred * centred, axis=-1, keepdims=True)) + 1e-06)
    normed_f = centred * rstd
    normed = (normed_f * norm_gain + norm_shift).astype(jnp.bfloat16).reshape(-1, width)
    pre = jnp.dot(normed, expand, preferred_element_type=jnp.float32) + expandbias
    cdf = 0.5 * (1.0 + lax.erf(pre * 0.7071067811865476))
    act = (pre * cdf).astype(jnp.bfloat16)
    out_branch = jnp.dot(act, project, preferred_element_type=jnp.float32) + projectbias
    cells = jnp.repeat(jnp.repeat(tile_valid, 8, axis=0), 8, axis=1).astype(jnp.float32)
    masked = (upstream.astype(jnp.float32) * cells[:, :, None]).reshape(-1, width)
    branch_grad = (masked * layer_scale).astype(jnp.bfloat16)
    act_grad = lax.dot_general(branch_grad, project, (((1,), (1,)), ((), ())), preferred_element_type=jnp.float32)
    slope = cdf + pre * jnp.exp(-0.5 * pre * pre) * 0.3989422804014327
    pre_grad = (act_grad * slope).astype(jnp.bfloat16)
    normed_grad = lax.dot_general(pre_grad, expand, (((1,), (1,)), ((), ())), preferred_element_type=jnp.float32).reshape(height, breadth, width)
    gained = normed_grad * norm_gain
    mixed_grad = (rstd * (gained - lax.optimization_barrier(jnp.mean(gained, axis=-1, keepdims=True)) - normed_f * lax.optimization_barrier(jnp.mean(gained * normed_f, axis=-1, keepdims=True)))).astype(jnp.bfloat16)
    grad_pad = jnp.pad(mixed_grad, ((3, 3), (3, 3), (0, 0)))
    back = depth_conv(grad_pad, depthwise[::-1, ::-1], height, breadth)
    features_grad = (masked.reshape(height, breadth, width) + back).astype(jnp.bfloat16)
    factor = float(NH * NW) ** (-0.5)
    grad_f = mixed_grad.astype(jnp.float32)
    depthwise_grad = kernel_sums(padded, grad_f, height, breadth) * factor
    depthbias_grad = lax.optimization_barrier(jnp.sum(grad_f, axis=(0, 1))) * factor
    gain_grad = lax.optimization_barrier(jnp.sum(normed_grad * normed_f, axis=(0, 1))) * factor
    shift_grad = lax.optimization_barrier(jnp.sum(normed_grad, axis=(0, 1))) * factor
    expand_grad = lax.dot_general(normed, pre_grad, (((0,), (0,)), ((), ())), preferred_element_type=jnp.float32) * factor
    expandbias_grad = lax.optimization_barrier(jnp.sum(pre_grad.astype(jnp.float32), axis=0)) * factor
    project_grad = lax.dot_general(act, branch_grad, (((0,), (0,)), ((), ())), preferred_element_type=jnp.float32) * factor
    projectbias_grad = lax.optimization_barrier(jnp.sum(branch_grad.astype(jnp.float32), axis=0)) * factor
    scale_grad = lax.optimization_barrier(jnp.sum(masked * out_branch, axis=0)) * factor
    return (features_grad, depthwise_grad, depthbias_grad, gain_grad, shift_grad, expand_grad, expandbias_grad, project_grad, projectbias_grad, scale_grad)
```

```python
import jax
import jax.numpy as jnp
from jax import lax
from jax.sharding import PartitionSpec as P


def with_halo(value, sides, width):
    for axis, dim in sides:
        size, length = (lax.axis_size(axis), value.shape[dim])
        up = [(i, (i + 1) % size) for i in range(size - 1)]
        down = [(j, i) for i, j in up]
        last = lax.slice_in_dim(value, length - width, length, axis=dim)
        initial = lax.slice_in_dim(value, 0, width, axis=dim)
        before = lax.ppermute(last, axis, up)
        after = lax.ppermute(initial, axis, down)
        value = jnp.concatenate([before, value, after], axis=dim)
    return value


def depth_conv(padded, depthwise, height, breadth):
    total = jnp.zeros((height, breadth, padded.shape[2]), jnp.float32)
    for row_off in range(7):
        for col_off in range(7):
            window = padded[row_off : row_off + height, col_off : col_off + breadth].astype(
                jnp.float32
            )
            total = total + window * depthwise[row_off, col_off].astype(jnp.float32)
    return total


def kernel_sums(padded, grad_cells, height, breadth):
    rows_out = []
    for row_off in range(7):
        for col_off in range(7):
            window = padded[row_off : row_off + height, col_off : col_off + breadth].astype(
                jnp.float32
            )
            rows_out.append(jnp.sum(window * grad_cells, axis=(0, 1)))
    return jnp.stack(rows_out).reshape(7, 7, grad_cells.shape[2])


def split_rows(row_count):
    low = 1
    while low * low * 4 <= row_count:
        low *= 2
    return row_count // low, low


def stage(value, axis, dim, size, place, perm_of):
    total = lax.dynamic_index_in_dim(value, place, dim, keepdims=False)
    for step in range(1, size):
        theirs = lax.dynamic_index_in_dim(value, (place + step) % size, dim, keepdims=False)
        got = lax.ppermute(theirs.astype(jnp.bfloat16), axis, perm_of(step))
        total = total + got.astype(jnp.float32)
    return total


def scatter_sum(partial):
    rows, cols = (lax.axis_size("rows"), lax.axis_size("cols"))
    high, low = split_rows(rows)
    row, col = (lax.axis_index("rows"), lax.axis_index("cols"))
    block = partial.shape[0] // (rows * cols)
    value = partial.reshape(high, low, cols, block, partial.shape[1])
    value = stage(
        value, "cols", 2, cols, col, lambda k: [(i, (i + k) % cols) for i in range(cols)]
    )
    value = stage(
        value,
        "rows",
        1,
        low,
        row % low,
        lambda k: [(i, i // low * low + (i % low + k) % low) for i in range(rows)],
    )
    return stage(
        value, "rows", 0, high, row // low, lambda k: [(i, (i + k * low) % rows) for i in range(rows)]
    )


def whole_sum(value):
    for axis in ("cols", "rows"):
        size = lax.axis_size(axis)
        bit = 1
        while bit < size:
            value = value + lax.ppermute(value, axis, [(i, i ^ bit) for i in range(size)])
            bit *= 2
    return value


def per_device(
    features,
    upstream,
    tile_valid,
    depthwise,
    depthbias,
    norm_gain,
    norm_shift,
    expand,
    expandbias,
    project,
    projectbias,
    layer_scale,
):
    height, breadth, width = features.shape
    row_count = lax.axis_size("rows")
    col_count = lax.axis_size("cols")
    padded = with_halo(features, (("rows", 0), ("cols", 1)), 3)
    mixed = depth_conv(padded, depthwise, height, breadth) + depthbias
    centred = mixed - jnp.mean(mixed, axis=-1, keepdims=True)
    rstd = lax.rsqrt(jnp.mean(centred * centred, axis=-1, keepdims=True) + 1e-06)
    normed_f = centred * rstd
    normed = (normed_f * norm_gain + norm_shift).astype(jnp.bfloat16).reshape(-1, width)
    pre = jnp.dot(normed, expand, preferred_element_type=jnp.float32) + expandbias
    cdf = 0.5 * (1.0 + lax.erf(pre * 0.7071067811865476))
    act = (pre * cdf).astype(jnp.bfloat16)
    out_branch = jnp.dot(act, project, preferred_element_type=jnp.float32) + projectbias
    row_cells = lax.axis_index("rows") * height + jnp.arange(height, dtype=jnp.int32)
    col_cells = lax.axis_index("cols") * breadth + jnp.arange(breadth, dtype=jnp.int32)
    row_pick = (
        row_cells[:, None] // 8 == jnp.arange(tile_valid.shape[0], dtype=jnp.int32)[None, :]
    ).astype(jnp.float32)
    col_pick = (
        col_cells[:, None] // 8 == jnp.arange(tile_valid.shape[1], dtype=jnp.int32)[None, :]
    ).astype(jnp.float32)
    row_tiles = jnp.dot(row_pick, tile_valid.astype(jnp.float32), precision=lax.Precision.HIGHEST)
    cells = lax.dot_general(
        row_tiles, col_pick, (((1,), (1,)), ((), ())), precision=lax.Precision.HIGHEST
    )
    masked = (upstream.astype(jnp.float32) * cells[:, :, None]).reshape(-1, width)
    branch_grad = (masked * layer_scale).astype(jnp.bfloat16)
    act_grad = lax.dot_general(
        branch_grad, project, (((1,), (1,)), ((), ())), preferred_element_type=jnp.float32
    )
    slope = cdf + pre * jnp.exp(-0.5 * pre * pre) * 0.3989422804014327
    pre_grad = (act_grad * slope).astype(jnp.bfloat16)
    normed_grad = lax.dot_general(
        pre_grad, expand, (((1,), (1,)), ((), ())), preferred_element_type=jnp.float32
    ).reshape(height, breadth, width)
    gained = normed_grad * norm_gain
    mixed_grad = (
        rstd
        * (
            gained
            - jnp.mean(gained, axis=-1, keepdims=True)
            - normed_f * jnp.mean(gained * normed_f, axis=-1, keepdims=True)
        )
    ).astype(jnp.bfloat16)
    grad_pad = with_halo(mixed_grad, (("rows", 0), ("cols", 1)), 3)
    back = depth_conv(grad_pad, depthwise[::-1, ::-1], height, breadth)
    features_grad = (masked.reshape(height, breadth, width) + back).astype(jnp.bfloat16)
    factor = float(height * row_count * breadth * col_count) ** (-0.5)
    expand_grad = scatter_sum(
        lax.dot_general(
            normed, pre_grad, (((0,), (0,)), ((), ())), preferred_element_type=jnp.float32
        )
        * factor
    )
    project_grad = scatter_sum(
        lax.dot_general(
            act, branch_grad, (((0,), (0,)), ((), ())), preferred_element_type=jnp.float32
        )
        * factor
    )
    grad_f = mixed_grad.astype(jnp.float32)
    local_sums = (
        kernel_sums(padded, grad_f, height, breadth),
        jnp.sum(grad_f, axis=(0, 1)),
        jnp.sum(normed_grad * normed_f, axis=(0, 1)),
        jnp.sum(normed_grad, axis=(0, 1)),
        jnp.sum(pre_grad.astype(jnp.float32), axis=0),
        jnp.sum(branch_grad.astype(jnp.float32), axis=0),
        jnp.sum(masked * out_branch, axis=0),
    )
    packed = jnp.concatenate([value.reshape(-1, width) for value in local_sums], axis=0)
    packed = whole_sum(packed) * factor
    hidden = expand.shape[1]
    depthwise_grad = packed[:49].reshape(7, 7, width)
    depthbias_grad = packed[49]
    gain_grad = packed[50]
    shift_grad = packed[51]
    expandbias_grad = packed[52 : 52 + hidden // width].reshape(hidden)
    projectbias_grad = packed[52 + hidden // width]
    scale_grad = packed[53 + hidden // width]
    return (
        features_grad,
        depthwise_grad,
        depthbias_grad,
        gain_grad,
        shift_grad,
        expand_grad,
        expandbias_grad,
        project_grad,
        projectbias_grad,
        scale_grad,
    )


def solution(mesh):
    return jax.shard_map(
        per_device,
        mesh=mesh,
        in_specs=(
            P(("groups", "rows"), "cols", None),
            P(("groups", "rows"), "cols", None),
            P("groups", None),
            P(),
            P(),
            P(),
            P(),
            P(),
            P(),
            P(),
            P(),
            P(),
        ),
        out_specs=(
            P(("groups", "rows"), "cols", None),
            P("groups", None, None),
            P("groups"),
            P("groups"),
            P("groups"),
            P(("groups", "rows", "cols"), None),
            P("groups"),
            P(("groups", "rows", "cols"), None),
            P("groups"),
            P("groups"),
        ),
        check_vma=False,
    )
```

```python
import jax
import jax.numpy as jnp
from jax import lax
from jax.experimental import pallas as pl
from jax.experimental.pallas import tpu as pltpu
from jax.sharding import PartitionSpec as P

MESH = pl.DeviceIdType.MESH
EDGE = 16
REACH = 3
TILE = 32
LANES = 128


class Halo:
    def __init__(self, own, pad, send, recv):
        height, breadth, _ = own.shape
        self.row, self.col = lax.axis_index("rows"), lax.axis_index("cols")
        self.rows = lax.axis_size("rows")
        self.own, self.pad = own, pad
        self.height, self.breadth = height, breadth
        row, other = self.row, 1 - self.col
        far = EDGE + breadth
        near = pl.ds(pl.multiple_of(other * (breadth - EDGE), EDGE), EDGE)
        there = pl.ds(pl.multiple_of(self.col * far, EDGE), EDGE)
        here = pl.ds(pl.multiple_of(other * far, EDGE), EDGE)
        mid = pl.ds(EDGE, breadth)
        full = pl.ds(0, breadth)
        top, bottom = pl.ds(0, REACH), pl.ds(REACH + height, REACH)
        first, last = pl.ds(0, REACH), pl.ds(height - REACH, REACH)
        inner, every = pl.ds(REACH, height), pl.ds(0, height)

        def pair(k, source, target, landing, device):
            def copy(spot):
                return pltpu.make_async_remote_copy(
                    src_ref=own.at[source[0], source[1]],
                    dst_ref=pad.at[spot[0], spot[1]],
                    send_sem=send.at[k],
                    recv_sem=recv.at[k],
                    device_id=device,
                    device_id_type=MESH,
                )

            return copy(target), copy(landing)

        up, down = ({"rows": row - 1}, {"rows": row + 1})
        self.edge = pair(0, (every, near), (inner, there), (inner, here), {"cols": other})
        self.to_next = (
            pair(1, (last, full), (top, mid), (top, mid), down),
            pair(3, (last, near), (top, there), (top, here), {**down, "cols": other}),
        )
        self.to_previous = (
            pair(2, (first, full), (bottom, mid), (bottom, mid), up),
            pair(4, (first, near), (bottom, there), (bottom, here), {**up, "cols": other}),
        )

    def start(self):
        row, rows, col = self.row, self.rows, self.col
        barrier = pltpu.get_barrier_semaphore()

        def greet(device):
            pl.semaphore_signal(barrier, inc=1, device_id=device, device_id_type=MESH)

        greet({"cols": 1 - col})

        @pl.when(row > 0)
        def _():
            greet({"rows": row - 1})
            greet({"rows": row - 1, "cols": 1 - col})

        @pl.when(row < rows - 1)
        def _():
            greet({"rows": row + 1})
            greet({"rows": row + 1, "cols": 1 - col})

        pl.semaphore_wait(
            barrier, 1 + 2 * (row > 0).astype(jnp.int32) + 2 * (row < rows - 1).astype(jnp.int32)
        )

        @pl.when(row < rows - 1)
        def _():
            for out, _ in self.to_next:
                out.start()

        @pl.when(row > 0)
        def _():
            for out, _ in self.to_previous:
                out.start()

        self.edge[0].start()
        pad, height, far = self.pad, self.height, EDGE + self.breadth

        def clear(rows_at, cols_at):
            shape = (rows_at.stop - rows_at.start, cols_at.stop - cols_at.start, pad.shape[2])
            pad[rows_at, cols_at, :] = jnp.zeros(shape, pad.dtype)

        @pl.when(col == 0)
        def _():
            clear(slice(0, pad.shape[0]), slice(0, EDGE))

        @pl.when(col == 1)
        def _():
            clear(slice(0, pad.shape[0]), slice(far, far + EDGE))

        for at_end, rows_at in (
            (row == 0, slice(0, REACH)),
            (row == rows - 1, slice(REACH + height, 2 * REACH + height)),
        ):

            @pl.when(at_end & (col == 0))
            def _():
                clear(rows_at, slice(EDGE, far + EDGE))

            @pl.when(at_end & (col == 1))
            def _():
                clear(rows_at, slice(0, far))

        pad[REACH : REACH + height, EDGE:far, :] = self.own[...]

    def wait_edge(self):
        self.edge[1].wait_recv()

    def wait_rows(self):
        @pl.when(self.row > 0)
        def _():
            for _, landed in self.to_next:
                landed.wait_recv()

        @pl.when(self.row < self.rows - 1)
        def _():
            for _, landed in self.to_previous:
                landed.wait_recv()

    def finish(self):
        self.edge[0].wait_send()

        @pl.when(self.row < self.rows - 1)
        def _():
            for out, _ in self.to_next:
                out.wait_send()

        @pl.when(self.row > 0)
        def _():
            for out, _ in self.to_previous:
                out.wait_send()


def over_lanes(width, body):
    def step(index, carry):
        body(pl.ds(pl.multiple_of(index * LANES, LANES), LANES))
        return carry

    lax.fori_loop(0, width // LANES, step, 0)


def conv_rows(pad, stage, weight, base, total, in_rows, finish):
    height, breadth, width = total.shape

    def chunk(lanes):
        for i in in_rows:
            stage[i] = pad[i, :, lanes].astype(jnp.float32)

        def tile(t, carry):
            start = pl.multiple_of(t * TILE, TILE)
            cells = pl.ds(start, TILE)
            sums = [base(r, cells, lanes) for r in range(height)]
            for b in range(7):
                for i in in_rows:
                    window = stage[i, pl.ds(start + EDGE - REACH + b, TILE), :]
                    for r in range(height):
                        if 0 <= i - r < 7:
                            tap = weight[pl.ds((i - r) * 7 + b, 1), lanes]
                            sums[r] = sums[r] + window * tap
            for r in range(height):
                total[r, cells, lanes] = finish(sums[r])
            return carry

        lax.fori_loop(0, breadth // TILE, tile, 0)

    over_lanes(width, chunk)


def sum_taps(pad, stage, grad, parts, out):
    height, breadth, width = grad.shape

    def chunk(lanes):
        for i in range(height + 2 * REACH):
            stage[i] = pad[i, :, lanes].astype(jnp.float32)
        parts[...] = jnp.zeros_like(parts)

        def tile(t, carry):
            start = pl.multiple_of(t * TILE, TILE)
            near = [
                grad[r, pl.ds(start, TILE), lanes].astype(jnp.float32) for r in range(height)
            ]
            for b in range(7):
                sums = [None] * 7
                for i in range(height + 2 * REACH):
                    window = stage[i, pl.ds(start + EDGE - REACH + b, TILE), :]
                    for r in range(height):
                        a = i - r
                        if 0 <= a < 7:
                            term = window * near[r]
                            sums[a] = term if sums[a] is None else sums[a] + term
                for a in range(7):
                    parts[7 * a + b] += jnp.sum(sums[a].reshape(TILE // 8, 8, LANES), axis=0)
            return carry

        lax.fori_loop(0, breadth // TILE, tile, 0)
        out[:, lanes] = jnp.sum(parts[...], axis=1)

    over_lanes(width, chunk)


def forward_kernel(own, weight, bias, mixed, pad_out, pad, stage, send, recv):
    height, _, _ = own.shape
    halo = Halo(own, pad, send, recv)
    halo.start()
    halo.wait_edge()
    same = lambda value: value
    start = lambda r, cells, lanes: jnp.broadcast_to(bias[:, lanes], (TILE, LANES))
    conv_rows(pad, stage, weight, start, mixed, range(REACH, REACH + height), same)
    halo.wait_rows()
    border = [*range(REACH), *range(REACH + height, 2 * REACH + height)]
    conv_rows(pad, stage, weight, lambda r, cells, lanes: mixed[r, cells, lanes], mixed, border, same)
    pad_out[...] = pad[...]
    halo.finish()


def backward_kernel(
    own, weight, masked, features, grad, taps, pad, stage, total, parts, send, recv
):
    height, _, _ = own.shape
    halo = Halo(own, pad, send, recv)
    halo.start()
    sum_taps(features, stage, own, parts, taps)
    halo.wait_edge()
    start = lambda r, cells, lanes: masked[r, cells, lanes]
    conv_rows(pad, stage, weight, start, total, range(REACH, REACH + height), lambda value: value)
    halo.wait_rows()
    border = [*range(REACH), *range(REACH + height, 2 * REACH + height)]
    start = lambda r, cells, lanes: total[r, cells, lanes]
    conv_rows(pad, stage, weight, start, grad, border, lambda value: value.astype(grad.dtype))
    halo.finish()


def halo_call(kernel, shape, outs, extra, ident, passes):
    height, breadth, width = shape
    vmem = pl.BlockSpec(memory_space=pltpu.VMEM)
    padded = (height + 2 * REACH, breadth + 2 * EDGE)
    flops = 98 * height * breadth * width * passes
    return pl.pallas_call(
        kernel,
        out_shape=outs,
        in_specs=[vmem] * (3 if ident == 0 else 4),
        out_specs=[vmem] * len(outs),
        scratch_shapes=[
            pltpu.VMEM((*padded, width), jnp.bfloat16),
            pltpu.VMEM((*padded, LANES), jnp.float32),
            *extra,
            pltpu.SemaphoreType.DMA((5,)),
            pltpu.SemaphoreType.DMA((5,)),
        ],
        compiler_params=pltpu.CompilerParams(
            collective_id=ident, has_side_effects=True, vmem_limit_bytes=48 * 1024 * 1024
        ),
        cost_estimate=pl.CostEstimate(flops=flops, bytes_accessed=8 * 1024 * 1024, transcendentals=0),
    )


def split_rows(row_count):
    low = 1
    while low * low * 4 <= row_count:
        low *= 2
    return row_count // low, low


def stage(value, axis, dim, size, place, perm_of):
    total = lax.dynamic_index_in_dim(value, place, dim, keepdims=False)
    for step in range(1, size):
        theirs = lax.dynamic_index_in_dim(value, (place + step) % size, dim, keepdims=False)
        got = lax.ppermute(theirs.astype(jnp.bfloat16), axis, perm_of(step))
        total = total + got.astype(jnp.float32)
    return total


def scatter_sum(partial):
    rows, cols = (lax.axis_size("rows"), lax.axis_size("cols"))
    high, low = split_rows(rows)
    row, col = (lax.axis_index("rows"), lax.axis_index("cols"))
    block = partial.shape[0] // (rows * cols)
    value = partial.reshape(high, low, cols, block, partial.shape[1])
    value = stage(
        value, "cols", 2, cols, col, lambda k: [(i, (i + k) % cols) for i in range(cols)]
    )
    value = stage(
        value,
        "rows",
        1,
        low,
        row % low,
        lambda k: [(i, i // low * low + (i % low + k) % low) for i in range(rows)],
    )
    return stage(
        value, "rows", 0, high, row // low, lambda k: [(i, (i + k * low) % rows) for i in range(rows)]
    )


def whole_sum(value):
    for axis in ("cols", "rows"):
        size = lax.axis_size(axis)
        bit = 1
        while bit < size:
            value = value + lax.ppermute(value, axis, [(i, i ^ bit) for i in range(size)])
            bit *= 2
    return value


def per_device(
    features,
    upstream,
    tile_valid,
    depthwise,
    depthbias,
    norm_gain,
    norm_shift,
    expand,
    expandbias,
    project,
    projectbias,
    layer_scale,
):
    height, breadth, width = features.shape
    row_count = lax.axis_size("rows")
    col_count = lax.axis_size("cols")
    taps = depthwise.astype(jnp.float32).reshape(49, width)
    padded_shape = (height + 2 * REACH, breadth + 2 * EDGE, width)
    mixed, padded = halo_call(
        forward_kernel,
        features.shape,
        [
            jax.ShapeDtypeStruct(features.shape, jnp.float32),
            jax.ShapeDtypeStruct(padded_shape, jnp.bfloat16),
        ],
        [],
        0,
        1,
    )(features, taps, depthbias[None])
    centred = mixed - jnp.mean(mixed, axis=-1, keepdims=True)
    rstd = lax.rsqrt(jnp.mean(centred * centred, axis=-1, keepdims=True) + 1e-06)
    normed_f = centred * rstd
    normed = (normed_f * norm_gain + norm_shift).astype(jnp.bfloat16).reshape(-1, width)
    pre = jnp.dot(normed, expand, preferred_element_type=jnp.float32) + expandbias
    cdf = 0.5 * (1.0 + lax.erf(pre * 0.7071067811865476))
    act = (pre * cdf).astype(jnp.bfloat16)
    out_branch = jnp.dot(act, project, preferred_element_type=jnp.float32) + projectbias
    row_cells = lax.axis_index("rows") * height + jnp.arange(height, dtype=jnp.int32)
    col_cells = lax.axis_index("cols") * breadth + jnp.arange(breadth, dtype=jnp.int32)
    row_pick = (
        row_cells[:, None] // 8 == jnp.arange(tile_valid.shape[0], dtype=jnp.int32)[None, :]
    ).astype(jnp.float32)
    col_pick = (
        col_cells[:, None] // 8 == jnp.arange(tile_valid.shape[1], dtype=jnp.int32)[None, :]
    ).astype(jnp.float32)
    row_tiles = jnp.dot(row_pick, tile_valid.astype(jnp.float32), precision=lax.Precision.HIGHEST)
    cells = lax.dot_general(
        row_tiles, col_pick, (((1,), (1,)), ((), ())), precision=lax.Precision.HIGHEST
    )
    masked = (upstream.astype(jnp.float32) * cells[:, :, None]).reshape(-1, width)
    branch_grad = (masked * layer_scale).astype(jnp.bfloat16)
    act_grad = lax.dot_general(
        branch_grad, project, (((1,), (1,)), ((), ())), preferred_element_type=jnp.float32
    )
    slope = cdf + pre * jnp.exp(-0.5 * pre * pre) * 0.3989422804014327
    pre_grad = (act_grad * slope).astype(jnp.bfloat16)
    normed_grad = lax.dot_general(
        pre_grad, expand, (((1,), (1,)), ((), ())), preferred_element_type=jnp.float32
    ).reshape(height, breadth, width)
    gained = normed_grad * norm_gain
    mixed_grad = (
        rstd
        * (
            gained
            - jnp.mean(gained, axis=-1, keepdims=True)
            - normed_f * jnp.mean(gained * normed_f, axis=-1, keepdims=True)
        )
    ).astype(jnp.bfloat16)
    features_grad, tap_sums = halo_call(
        backward_kernel,
        features.shape,
        [
            jax.ShapeDtypeStruct(features.shape, jnp.bfloat16),
            jax.ShapeDtypeStruct((49, width), jnp.float32),
        ],
        [
            pltpu.VMEM(features.shape, jnp.float32),
            pltpu.VMEM((49, 8, LANES), jnp.float32),
        ],
        1,
        2,
    )(mixed_grad, taps[::-1], masked.reshape(height, breadth, width), padded)
    factor = float(height * row_count * breadth * col_count) ** (-0.5)
    expand_grad = scatter_sum(
        lax.dot_general(
            normed, pre_grad, (((0,), (0,)), ((), ())), preferred_element_type=jnp.float32
        )
        * factor
    )
    project_grad = scatter_sum(
        lax.dot_general(
            act, branch_grad, (((0,), (0,)), ((), ())), preferred_element_type=jnp.float32
        )
        * factor
    )
    grad_f = mixed_grad.astype(jnp.float32)
    local_sums = (
        tap_sums,
        jnp.sum(grad_f, axis=(0, 1)),
        jnp.sum(normed_grad * normed_f, axis=(0, 1)),
        jnp.sum(normed_grad, axis=(0, 1)),
        jnp.sum(pre_grad.astype(jnp.float32), axis=0),
        jnp.sum(branch_grad.astype(jnp.float32), axis=0),
        jnp.sum(masked * out_branch, axis=0),
    )
    packed = jnp.concatenate([value.reshape(-1, width) for value in local_sums], axis=0)
    packed = whole_sum(packed) * factor
    hidden = expand.shape[1]
    depthwise_grad = packed[:49].reshape(7, 7, width)
    depthbias_grad = packed[49]
    gain_grad = packed[50]
    shift_grad = packed[51]
    expandbias_grad = packed[52 : 52 + hidden // width].reshape(hidden)
    projectbias_grad = packed[52 + hidden // width]
    scale_grad = packed[53 + hidden // width]
    return (
        features_grad,
        depthwise_grad,
        depthbias_grad,
        gain_grad,
        shift_grad,
        expand_grad,
        expandbias_grad,
        project_grad,
        projectbias_grad,
        scale_grad,
    )


def solution(mesh):
    return jax.shard_map(
        per_device,
        mesh=mesh,
        in_specs=(
            P(("groups", "rows"), "cols", None),
            P(("groups", "rows"), "cols", None),
            P("groups", None),
            P(),
            P(),
            P(),
            P(),
            P(),
            P(),
            P(),
            P(),
            P(),
        ),
        out_specs=(
            P(("groups", "rows"), "cols", None),
            P("groups", None, None),
            P("groups"),
            P("groups"),
            P("groups"),
            P(("groups", "rows", "cols"), None),
            P("groups"),
            P(("groups", "rows", "cols"), None),
            P("groups"),
            P("groups"),
        ),
        check_vma=False,
    )
```

```python
import jax
import jax.numpy as jnp
from jax import lax
from jax.experimental import pallas as pl
from jax.experimental.pallas import tpu as pltpu
from jax.sharding import PartitionSpec as P

MESH = pl.DeviceIdType.MESH
EDGE = 16
REACH = 3
TILE = 32
LANES = 128


class Halo:
    def __init__(self, own, pad, send, recv):
        height, breadth, _ = own.shape
        self.row, self.col = lax.axis_index("rows"), lax.axis_index("cols")
        self.rows = lax.axis_size("rows")
        self.own, self.pad = own, pad
        self.height, self.breadth = height, breadth
        row, other = self.row, 1 - self.col
        far = EDGE + breadth
        near = pl.ds(pl.multiple_of(other * (breadth - EDGE), EDGE), EDGE)
        there = pl.ds(pl.multiple_of(self.col * far, EDGE), EDGE)
        here = pl.ds(pl.multiple_of(other * far, EDGE), EDGE)
        mid = pl.ds(EDGE, breadth)
        full = pl.ds(0, breadth)
        top, bottom = pl.ds(0, REACH), pl.ds(REACH + height, REACH)
        first, last = pl.ds(0, REACH), pl.ds(height - REACH, REACH)
        inner, every = pl.ds(REACH, height), pl.ds(0, height)

        def pair(k, source, target, landing, device):
            def copy(spot):
                return pltpu.make_async_remote_copy(
                    src_ref=own.at[source[0], source[1]],
                    dst_ref=pad.at[spot[0], spot[1]],
                    send_sem=send.at[k],
                    recv_sem=recv.at[k],
                    device_id=device,
                    device_id_type=MESH,
                )

            return copy(target), copy(landing)

        up, down = ({"rows": row - 1}, {"rows": row + 1})
        self.edge = pair(0, (every, near), (inner, there), (inner, here), {"cols": other})
        self.to_next = (
            pair(1, (last, full), (top, mid), (top, mid), down),
            pair(3, (last, near), (top, there), (top, here), {**down, "cols": other}),
        )
        self.to_previous = (
            pair(2, (first, full), (bottom, mid), (bottom, mid), up),
            pair(4, (first, near), (bottom, there), (bottom, here), {**up, "cols": other}),
        )

    def start(self):
        row, rows, col = self.row, self.rows, self.col
        barrier = pltpu.get_barrier_semaphore()

        def greet(device):
            pl.semaphore_signal(barrier, inc=1, device_id=device, device_id_type=MESH)

        greet({"cols": 1 - col})

        @pl.when(row > 0)
        def _():
            greet({"rows": row - 1})
            greet({"rows": row - 1, "cols": 1 - col})

        @pl.when(row < rows - 1)
        def _():
            greet({"rows": row + 1})
            greet({"rows": row + 1, "cols": 1 - col})

        pl.semaphore_wait(
            barrier, 1 + 2 * (row > 0).astype(jnp.int32) + 2 * (row < rows - 1).astype(jnp.int32)
        )

        @pl.when(row < rows - 1)
        def _():
            for out, _ in self.to_next:
                out.start()

        @pl.when(row > 0)
        def _():
            for out, _ in self.to_previous:
                out.start()

        self.edge[0].start()
        pad, height, far = self.pad, self.height, EDGE + self.breadth

        def clear(rows_at, cols_at):
            shape = (rows_at.stop - rows_at.start, cols_at.stop - cols_at.start, pad.shape[2])
            pad[rows_at, cols_at, :] = jnp.zeros(shape, pad.dtype)

        @pl.when(col == 0)
        def _():
            clear(slice(0, pad.shape[0]), slice(0, EDGE))

        @pl.when(col == 1)
        def _():
            clear(slice(0, pad.shape[0]), slice(far, far + EDGE))

        for at_end, rows_at in (
            (row == 0, slice(0, REACH)),
            (row == rows - 1, slice(REACH + height, 2 * REACH + height)),
        ):

            @pl.when(at_end & (col == 0))
            def _():
                clear(rows_at, slice(EDGE, far + EDGE))

            @pl.when(at_end & (col == 1))
            def _():
                clear(rows_at, slice(0, far))

        pad[REACH : REACH + height, EDGE:far, :] = self.own[...]

    def wait_edge(self):
        self.edge[1].wait_recv()

    def wait_rows(self):
        @pl.when(self.row > 0)
        def _():
            for _, landed in self.to_next:
                landed.wait_recv()

        @pl.when(self.row < self.rows - 1)
        def _():
            for _, landed in self.to_previous:
                landed.wait_recv()

    def finish(self):
        self.edge[0].wait_send()

        @pl.when(self.row < self.rows - 1)
        def _():
            for out, _ in self.to_next:
                out.wait_send()

        @pl.when(self.row > 0)
        def _():
            for out, _ in self.to_previous:
                out.wait_send()


def over_lanes(width, body):
    def step(index, carry):
        body(pl.ds(pl.multiple_of(index * LANES, LANES), LANES))
        return carry

    lax.fori_loop(0, width // LANES, step, 0)


def conv_rows(pad, stage, weight, base, total, in_rows, finish):
    height, breadth, width = total.shape

    def chunk(lanes):
        for i in in_rows:
            stage[i] = pad[i, :, lanes].astype(jnp.float32)

        def tile(t, carry):
            start = pl.multiple_of(t * TILE, TILE)
            cells = pl.ds(start, TILE)
            sums = [base(r, cells, lanes) for r in range(height)]
            for b in range(7):
                for i in in_rows:
                    window = stage[i, pl.ds(start + EDGE - REACH + b, TILE), :]
                    for r in range(height):
                        if 0 <= i - r < 7:
                            tap = weight[pl.ds((i - r) * 7 + b, 1), lanes]
                            sums[r] = sums[r] + window * tap
            for r in range(height):
                total[r, cells, lanes] = finish(sums[r])
            return carry

        lax.fori_loop(0, breadth // TILE, tile, 0)

    over_lanes(width, chunk)


def sum_taps(pad, stage, grad, parts, out):
    height, breadth, width = grad.shape

    def chunk(lanes):
        for i in range(height + 2 * REACH):
            stage[i] = pad[i, :, lanes].astype(jnp.float32)
        parts[...] = jnp.zeros_like(parts)

        def tile(t, carry):
            start = pl.multiple_of(t * TILE, TILE)
            near = [
                grad[r, pl.ds(start, TILE), lanes].astype(jnp.float32) for r in range(height)
            ]
            for b in range(7):
                sums = [None] * 7
                for i in range(height + 2 * REACH):
                    window = stage[i, pl.ds(start + EDGE - REACH + b, TILE), :]
                    for r in range(height):
                        a = i - r
                        if 0 <= a < 7:
                            term = window * near[r]
                            sums[a] = term if sums[a] is None else sums[a] + term
                for a in range(7):
                    parts[7 * a + b] += jnp.sum(sums[a].reshape(TILE // 8, 8, LANES), axis=0)
            return carry

        lax.fori_loop(0, breadth // TILE, tile, 0)
        out[:, lanes] = jnp.sum(parts[...], axis=1)

    over_lanes(width, chunk)


def forward_kernel(own, weight, bias, mixed, pad_out, pad, stage, send, recv):
    height, _, _ = own.shape
    halo = Halo(own, pad, send, recv)
    halo.start()
    halo.wait_edge()
    same = lambda value: value
    start = lambda r, cells, lanes: jnp.broadcast_to(bias[:, lanes], (TILE, LANES))
    conv_rows(pad, stage, weight, start, mixed, range(REACH, REACH + height), same)
    halo.wait_rows()
    border = [*range(REACH), *range(REACH + height, 2 * REACH + height)]
    conv_rows(pad, stage, weight, lambda r, cells, lanes: mixed[r, cells, lanes], mixed, border, same)
    pad_out[...] = pad[...]
    halo.finish()


def backward_kernel(
    own, weight, masked, features, grad, taps, pad, stage, total, parts, send, recv
):
    height, _, _ = own.shape
    halo = Halo(own, pad, send, recv)
    halo.start()
    sum_taps(features, stage, own, parts, taps)
    halo.wait_edge()
    start = lambda r, cells, lanes: masked[r, cells, lanes]
    conv_rows(pad, stage, weight, start, total, range(REACH, REACH + height), lambda value: value)
    halo.wait_rows()
    border = [*range(REACH), *range(REACH + height, 2 * REACH + height)]
    start = lambda r, cells, lanes: total[r, cells, lanes]
    conv_rows(pad, stage, weight, start, grad, border, lambda value: value.astype(grad.dtype))
    halo.finish()


def halo_call(kernel, shape, outs, extra, ident, passes):
    height, breadth, width = shape
    vmem = pl.BlockSpec(memory_space=pltpu.VMEM)
    padded = (height + 2 * REACH, breadth + 2 * EDGE)
    flops = 98 * height * breadth * width * passes
    return pl.pallas_call(
        kernel,
        out_shape=outs,
        in_specs=[vmem] * (3 if ident == 0 else 4),
        out_specs=[vmem] * len(outs),
        scratch_shapes=[
            pltpu.VMEM((*padded, width), jnp.bfloat16),
            pltpu.VMEM((*padded, LANES), jnp.float32),
            *extra,
            pltpu.SemaphoreType.DMA((5,)),
            pltpu.SemaphoreType.DMA((5,)),
        ],
        compiler_params=pltpu.CompilerParams(
            collective_id=ident, has_side_effects=True, vmem_limit_bytes=48 * 1024 * 1024
        ),
        cost_estimate=pl.CostEstimate(flops=flops, bytes_accessed=8 * 1024 * 1024, transcendentals=0),
    )


def split_rows(row_count):
    low = 1
    while low * low * 4 <= row_count:
        low *= 2
    return row_count // low, low


def pick(value, dim, size, place):
    own = lax.dynamic_index_in_dim(value, place, dim, keepdims=False)
    theirs = [
        lax.dynamic_index_in_dim(value, (place + step) % size, dim, keepdims=False).astype(
            jnp.bfloat16
        )
        for step in range(1, size)
    ]
    return own, theirs


def exchange(own, theirs, axis, perm_of):
    for step, part in enumerate(theirs, 1):
        own = own + lax.ppermute(part, axis, perm_of(step)).astype(jnp.float32)
    return own


def over_cores(partial):
    rows, cols = (lax.axis_size("rows"), lax.axis_size("cols"))
    high, low = split_rows(rows)
    block = partial.shape[0] // (rows * cols)
    value = partial.reshape(high, low, cols, block, partial.shape[1])
    own, theirs = pick(value, 2, cols, lax.axis_index("cols"))
    value = exchange(own, theirs, "cols", lambda k: [(i, (i + k) % cols) for i in range(cols)])
    return pick(value, 1, low, lax.axis_index("rows") % low)


def over_low(own, theirs):
    rows = lax.axis_size("rows")
    high, low = split_rows(rows)
    value = exchange(
        own,
        theirs,
        "rows",
        lambda k: [(i, i // low * low + (i % low + k) % low) for i in range(rows)],
    )
    return pick(value, 0, high, lax.axis_index("rows") // low)


def over_high(own, theirs):
    rows = lax.axis_size("rows")
    _, low = split_rows(rows)
    return exchange(own, theirs, "rows", lambda k: [(i, (i + k * low) % rows) for i in range(rows)])


def whole_sum(value):
    for axis in ("cols", "rows"):
        size = lax.axis_size(axis)
        bit = 1
        while bit < size:
            value = value + lax.ppermute(value, axis, [(i, i ^ bit) for i in range(size)])
            bit *= 2
    return value


def per_device(
    features,
    upstream,
    tile_valid,
    depthwise,
    depthbias,
    norm_gain,
    norm_shift,
    expand,
    expandbias,
    project,
    projectbias,
    layer_scale,
):
    height, breadth, width = features.shape
    row_count = lax.axis_size("rows")
    col_count = lax.axis_size("cols")
    taps = depthwise.astype(jnp.float32).reshape(49, width)
    padded_shape = (height + 2 * REACH, breadth + 2 * EDGE, width)
    mixed, padded = halo_call(
        forward_kernel,
        features.shape,
        [
            jax.ShapeDtypeStruct(features.shape, jnp.float32),
            jax.ShapeDtypeStruct(padded_shape, jnp.bfloat16),
        ],
        [],
        0,
        1,
    )(features, taps, depthbias[None])
    centred = mixed - jnp.mean(mixed, axis=-1, keepdims=True)
    rstd = lax.rsqrt(jnp.mean(centred * centred, axis=-1, keepdims=True) + 1e-06)
    normed_f = centred * rstd
    normed = (normed_f * norm_gain + norm_shift).astype(jnp.bfloat16).reshape(-1, width)
    pre = jnp.dot(normed, expand, preferred_element_type=jnp.float32) + expandbias
    cdf = 0.5 * (1.0 + lax.erf(pre * 0.7071067811865476))
    act = (pre * cdf).astype(jnp.bfloat16)
    out_branch = jnp.dot(act, project, preferred_element_type=jnp.float32) + projectbias
    row_cells = lax.axis_index("rows") * height + jnp.arange(height, dtype=jnp.int32)
    col_cells = lax.axis_index("cols") * breadth + jnp.arange(breadth, dtype=jnp.int32)
    row_pick = (
        row_cells[:, None] // 8 == jnp.arange(tile_valid.shape[0], dtype=jnp.int32)[None, :]
    ).astype(jnp.float32)
    col_pick = (
        col_cells[:, None] // 8 == jnp.arange(tile_valid.shape[1], dtype=jnp.int32)[None, :]
    ).astype(jnp.float32)
    row_tiles = jnp.dot(row_pick, tile_valid.astype(jnp.float32), precision=lax.Precision.HIGHEST)
    cells = lax.dot_general(
        row_tiles, col_pick, (((1,), (1,)), ((), ())), precision=lax.Precision.HIGHEST
    )
    masked = (upstream.astype(jnp.float32) * cells[:, :, None]).reshape(-1, width)
    branch_grad = (masked * layer_scale).astype(jnp.bfloat16)
    act_grad = lax.dot_general(
        branch_grad, project, (((1,), (1,)), ((), ())), preferred_element_type=jnp.float32
    )
    slope = cdf + pre * jnp.exp(-0.5 * pre * pre) * 0.3989422804014327
    pre_grad = (act_grad * slope).astype(jnp.bfloat16)
    normed_grad = lax.dot_general(
        pre_grad, expand, (((1,), (1,)), ((), ())), preferred_element_type=jnp.float32
    ).reshape(height, breadth, width)
    gained = normed_grad * norm_gain
    mixed_grad = (
        rstd
        * (
            gained
            - jnp.mean(gained, axis=-1, keepdims=True)
            - normed_f * jnp.mean(gained * normed_f, axis=-1, keepdims=True)
        )
    ).astype(jnp.bfloat16)
    factor = float(height * row_count * breadth * col_count) ** (-0.5)
    project_low, project_sent = over_cores(
        lax.dot_general(
            act, branch_grad, (((0,), (0,)), ((), ())), preferred_element_type=jnp.float32
        )
        * factor
    )
    expand_low, expand_sent = over_cores(
        lax.dot_general(
            normed, pre_grad, (((0,), (0,)), ((), ())), preferred_element_type=jnp.float32
        )
        * factor
    )
    mixed_grad, project_sent, expand_sent = lax.optimization_barrier(
        (mixed_grad, project_sent, expand_sent)
    )
    features_grad, tap_sums = halo_call(
        backward_kernel,
        features.shape,
        [
            jax.ShapeDtypeStruct(features.shape, jnp.bfloat16),
            jax.ShapeDtypeStruct((49, width), jnp.float32),
        ],
        [
            pltpu.VMEM(features.shape, jnp.float32),
            pltpu.VMEM((49, 8, LANES), jnp.float32),
        ],
        1,
        2,
    )(mixed_grad, taps[::-1], masked.reshape(height, breadth, width), padded)
    grad_f = mixed_grad.astype(jnp.float32)
    local_sums = (
        tap_sums,
        jnp.sum(grad_f, axis=(0, 1)),
        jnp.sum(normed_grad * normed_f, axis=(0, 1)),
        jnp.sum(normed_grad, axis=(0, 1)),
        jnp.sum(pre_grad.astype(jnp.float32), axis=0),
        jnp.sum(branch_grad.astype(jnp.float32), axis=0),
        jnp.sum(masked * out_branch, axis=0),
    )
    packed = jnp.concatenate([value.reshape(-1, width) for value in local_sums], axis=0)
    project_high, project_sent = over_low(project_low, project_sent)
    expand_high, expand_sent = over_low(expand_low, expand_sent)
    packed, project_sent, expand_sent = lax.optimization_barrier(
        (packed, project_sent, expand_sent)
    )
    packed = whole_sum(packed) * factor
    project_grad = over_high(project_high, project_sent)
    expand_grad = over_high(expand_high, expand_sent)
    hidden = expand.shape[1]
    depthwise_grad = packed[:49].reshape(7, 7, width)
    depthbias_grad = packed[49]
    gain_grad = packed[50]
    shift_grad = packed[51]
    expandbias_grad = packed[52 : 52 + hidden // width].reshape(hidden)
    projectbias_grad = packed[52 + hidden // width]
    scale_grad = packed[53 + hidden // width]
    return (
        features_grad,
        depthwise_grad,
        depthbias_grad,
        gain_grad,
        shift_grad,
        expand_grad,
        expandbias_grad,
        project_grad,
        projectbias_grad,
        scale_grad,
    )


def solution(mesh):
    return jax.shard_map(
        per_device,
        mesh=mesh,
        in_specs=(
            P(("groups", "rows"), "cols", None),
            P(("groups", "rows"), "cols", None),
            P("groups", None),
            P(),
            P(),
            P(),
            P(),
            P(),
            P(),
            P(),
            P(),
            P(),
        ),
        out_specs=(
            P(("groups", "rows"), "cols", None),
            P("groups", None, None),
            P("groups"),
            P("groups"),
            P("groups"),
            P(("groups", "rows", "cols"), None),
            P("groups"),
            P(("groups", "rows", "cols"), None),
            P("groups"),
            P("groups"),
        ),
        check_vma=False,
    )
```

```python
import jax
import jax.numpy as jnp
from jax import lax
from jax.experimental import pallas as pl
from jax.experimental.pallas import tpu as pltpu
from jax.sharding import PartitionSpec as P

MESH = pl.DeviceIdType.MESH
EDGE = 16
REACH = 3
TILE = 32
LANES = 128


class Halo:
    def __init__(self, own, pad, send, recv):
        height, breadth, _ = own.shape
        self.row, self.col = lax.axis_index("rows"), lax.axis_index("cols")
        self.rows = lax.axis_size("rows")
        self.own, self.pad = own, pad
        self.height, self.breadth = height, breadth
        row, other = self.row, 1 - self.col
        far = EDGE + breadth
        near = pl.ds(pl.multiple_of(other * (breadth - EDGE), EDGE), EDGE)
        there = pl.ds(pl.multiple_of(self.col * far, EDGE), EDGE)
        here = pl.ds(pl.multiple_of(other * far, EDGE), EDGE)
        mid = pl.ds(EDGE, breadth)
        full = pl.ds(0, breadth)
        top, bottom = pl.ds(0, REACH), pl.ds(REACH + height, REACH)
        first, last = pl.ds(0, REACH), pl.ds(height - REACH, REACH)
        inner, every = pl.ds(REACH, height), pl.ds(0, height)

        def pair(k, source, target, landing, device):
            def copy(spot):
                return pltpu.make_async_remote_copy(
                    src_ref=own.at[source[0], source[1]],
                    dst_ref=pad.at[spot[0], spot[1]],
                    send_sem=send.at[k],
                    recv_sem=recv.at[k],
                    device_id=device,
                    device_id_type=MESH,
                )

            return copy(target), copy(landing)

        up, down = ({"rows": row - 1}, {"rows": row + 1})
        self.edge = pair(0, (every, near), (inner, there), (inner, here), {"cols": other})
        self.to_next = (
            pair(1, (last, full), (top, mid), (top, mid), down),
            pair(3, (last, near), (top, there), (top, here), {**down, "cols": other}),
        )
        self.to_previous = (
            pair(2, (first, full), (bottom, mid), (bottom, mid), up),
            pair(4, (first, near), (bottom, there), (bottom, here), {**up, "cols": other}),
        )

    def start(self):
        row, rows, col = self.row, self.rows, self.col
        barrier = pltpu.get_barrier_semaphore()

        def greet(device):
            pl.semaphore_signal(barrier, inc=1, device_id=device, device_id_type=MESH)

        greet({"cols": 1 - col})

        @pl.when(row > 0)
        def _():
            greet({"rows": row - 1})
            greet({"rows": row - 1, "cols": 1 - col})

        @pl.when(row < rows - 1)
        def _():
            greet({"rows": row + 1})
            greet({"rows": row + 1, "cols": 1 - col})

        pl.semaphore_wait(
            barrier, 1 + 2 * (row > 0).astype(jnp.int32) + 2 * (row < rows - 1).astype(jnp.int32)
        )

        @pl.when(row < rows - 1)
        def _():
            for out, _ in self.to_next:
                out.start()

        @pl.when(row > 0)
        def _():
            for out, _ in self.to_previous:
                out.start()

        self.edge[0].start()
        pad, height, far = self.pad, self.height, EDGE + self.breadth

        def clear(rows_at, cols_at):
            shape = (rows_at.stop - rows_at.start, cols_at.stop - cols_at.start, pad.shape[2])
            pad[rows_at, cols_at, :] = jnp.zeros(shape, pad.dtype)

        @pl.when(col == 0)
        def _():
            clear(slice(0, pad.shape[0]), slice(0, EDGE))

        @pl.when(col == 1)
        def _():
            clear(slice(0, pad.shape[0]), slice(far, far + EDGE))

        for at_end, rows_at in (
            (row == 0, slice(0, REACH)),
            (row == rows - 1, slice(REACH + height, 2 * REACH + height)),
        ):

            @pl.when(at_end & (col == 0))
            def _():
                clear(rows_at, slice(EDGE, far + EDGE))

            @pl.when(at_end & (col == 1))
            def _():
                clear(rows_at, slice(0, far))

        pad[REACH : REACH + height, EDGE:far, :] = self.own[...]

    def wait_edge(self):
        self.edge[1].wait_recv()

    def wait_rows(self):
        @pl.when(self.row > 0)
        def _():
            for _, landed in self.to_next:
                landed.wait_recv()

        @pl.when(self.row < self.rows - 1)
        def _():
            for _, landed in self.to_previous:
                landed.wait_recv()

    def finish(self):
        self.edge[0].wait_send()

        @pl.when(self.row < self.rows - 1)
        def _():
            for out, _ in self.to_next:
                out.wait_send()

        @pl.when(self.row > 0)
        def _():
            for out, _ in self.to_previous:
                out.wait_send()


def over_lanes(width, body):
    def step(index, carry):
        body(pl.ds(pl.multiple_of(index * LANES, LANES), LANES))
        return carry

    lax.fori_loop(0, width // LANES, step, 0)


def conv_rows(pad, stage, weight, base, total, in_rows, finish):
    height, breadth, width = total.shape

    def chunk(lanes):
        for i in in_rows:
            stage[i] = pad[i, :, lanes].astype(jnp.float32)

        def tile(t, carry):
            start = pl.multiple_of(t * TILE, TILE)
            cells = pl.ds(start, TILE)
            sums = [base(r, cells, lanes) for r in range(height)]
            for b in range(7):
                for i in in_rows:
                    window = stage[i, pl.ds(start + EDGE - REACH + b, TILE), :]
                    for r in range(height):
                        if 0 <= i - r < 7:
                            tap = weight[pl.ds((i - r) * 7 + b, 1), lanes]
                            sums[r] = sums[r] + window * tap
            for r in range(height):
                total[r, cells, lanes] = finish(sums[r])
            return carry

        lax.fori_loop(0, breadth // TILE, tile, 0)

    over_lanes(width, chunk)


def sum_taps(pad, stage, grad, parts, out):
    height, breadth, width = grad.shape

    def chunk(lanes):
        for i in range(height + 2 * REACH):
            stage[i] = pad[i, :, lanes].astype(jnp.float32)
        parts[...] = jnp.zeros_like(parts)

        def tile(t, carry):
            start = pl.multiple_of(t * TILE, TILE)
            near = [
                grad[r, pl.ds(start, TILE), lanes].astype(jnp.float32) for r in range(height)
            ]
            for b in range(7):
                sums = [None] * 7
                for i in range(height + 2 * REACH):
                    window = stage[i, pl.ds(start + EDGE - REACH + b, TILE), :]
                    for r in range(height):
                        a = i - r
                        if 0 <= a < 7:
                            term = window * near[r]
                            sums[a] = term if sums[a] is None else sums[a] + term
                for a in range(7):
                    parts[7 * a + b] += jnp.sum(sums[a].reshape(TILE // 8, 8, LANES), axis=0)
            return carry

        lax.fori_loop(0, breadth // TILE, tile, 0)
        out[:, lanes] = jnp.sum(parts[...], axis=1)

    over_lanes(width, chunk)


def forward_kernel(own, weight, bias, mixed, pad_out, pad, stage, send, recv):
    height, _, _ = own.shape
    halo = Halo(own, pad, send, recv)
    halo.start()
    halo.wait_edge()
    same = lambda value: value
    start = lambda r, cells, lanes: jnp.broadcast_to(bias[:, lanes], (TILE, LANES))
    conv_rows(pad, stage, weight, start, mixed, range(REACH, REACH + height), same)
    halo.wait_rows()
    border = [*range(REACH), *range(REACH + height, 2 * REACH + height)]
    conv_rows(pad, stage, weight, lambda r, cells, lanes: mixed[r, cells, lanes], mixed, border, same)
    pad_out[...] = pad[...]
    halo.finish()


def backward_kernel(
    own, weight, masked, features, grad, taps, pad, stage, total, parts, send, recv
):
    height, _, _ = own.shape
    halo = Halo(own, pad, send, recv)
    halo.start()
    sum_taps(features, stage, own, parts, taps)
    halo.wait_edge()
    start = lambda r, cells, lanes: masked[r, cells, lanes]
    conv_rows(pad, stage, weight, start, total, range(REACH, REACH + height), lambda value: value)
    halo.wait_rows()
    border = [*range(REACH), *range(REACH + height, 2 * REACH + height)]
    start = lambda r, cells, lanes: total[r, cells, lanes]
    conv_rows(pad, stage, weight, start, grad, border, lambda value: value.astype(grad.dtype))
    halo.finish()


def halo_call(kernel, shape, outs, extra, ident, passes):
    height, breadth, width = shape
    vmem = pl.BlockSpec(memory_space=pltpu.VMEM)
    padded = (height + 2 * REACH, breadth + 2 * EDGE)
    flops = 98 * height * breadth * width * passes
    return pl.pallas_call(
        kernel,
        out_shape=outs,
        in_specs=[vmem] * (3 if ident == 0 else 4),
        out_specs=[vmem] * len(outs),
        scratch_shapes=[
            pltpu.VMEM((*padded, width), jnp.bfloat16),
            pltpu.VMEM((*padded, LANES), jnp.float32),
            *extra,
            pltpu.SemaphoreType.DMA((5,)),
            pltpu.SemaphoreType.DMA((5,)),
        ],
        compiler_params=pltpu.CompilerParams(
            collective_id=ident, has_side_effects=True, vmem_limit_bytes=48 * 1024 * 1024
        ),
        cost_estimate=pl.CostEstimate(flops=flops, bytes_accessed=8 * 1024 * 1024, transcendentals=0),
    )


def split_rows(row_count):
    low = 1
    while low * low * 4 <= row_count:
        low *= 2
    return row_count // low, low


def pick(value, dim, size, place):
    own = lax.dynamic_index_in_dim(value, place, dim, keepdims=False)
    theirs = [
        lax.dynamic_index_in_dim(value, (place + step) % size, dim, keepdims=False).astype(
            jnp.bfloat16
        )
        for step in range(1, size)
    ]
    return own, theirs


def exchange(own, theirs, axis, perm_of):
    for step, part in enumerate(theirs, 1):
        own = own + lax.ppermute(part, axis, perm_of(step)).astype(jnp.float32)
    return own


def over_cores(partial, high_first):
    rows, cols = (lax.axis_size("rows"), lax.axis_size("cols"))
    high, low = split_rows(rows)
    block = partial.shape[0] // (rows * cols)
    value = partial.reshape(high, low, cols, block, partial.shape[1])
    own, theirs = pick(value, 2, cols, lax.axis_index("cols"))
    value = exchange(own, theirs, "cols", lambda k: [(i, (i + k) % cols) for i in range(cols)])
    if high_first:
        return pick(value, 0, high, lax.axis_index("rows") // low)
    return pick(value, 1, low, lax.axis_index("rows") % low)


def over_low(own, theirs):
    rows = lax.axis_size("rows")
    _, low = split_rows(rows)
    return exchange(
        own,
        theirs,
        "rows",
        lambda k: [(i, i // low * low + (i % low + k) % low) for i in range(rows)],
    )


def over_high(own, theirs):
    rows = lax.axis_size("rows")
    _, low = split_rows(rows)
    return exchange(own, theirs, "rows", lambda k: [(i, (i + k * low) % rows) for i in range(rows)])


def whole_sum(value):
    for axis in ("cols", "rows"):
        size = lax.axis_size(axis)
        bit = 1
        while bit < size:
            value = value + lax.ppermute(value, axis, [(i, i ^ bit) for i in range(size)])
            bit *= 2
    return value


def per_device(
    features,
    upstream,
    tile_valid,
    depthwise,
    depthbias,
    norm_gain,
    norm_shift,
    expand,
    expandbias,
    project,
    projectbias,
    layer_scale,
):
    height, breadth, width = features.shape
    row_count = lax.axis_size("rows")
    col_count = lax.axis_size("cols")
    taps = depthwise.astype(jnp.float32).reshape(49, width)
    padded_shape = (height + 2 * REACH, breadth + 2 * EDGE, width)
    mixed, padded = halo_call(
        forward_kernel,
        features.shape,
        [
            jax.ShapeDtypeStruct(features.shape, jnp.float32),
            jax.ShapeDtypeStruct(padded_shape, jnp.bfloat16),
        ],
        [],
        0,
        1,
    )(features, taps, depthbias[None])
    centred = mixed - jnp.mean(mixed, axis=-1, keepdims=True)
    rstd = lax.rsqrt(jnp.mean(centred * centred, axis=-1, keepdims=True) + 1e-06)
    normed_f = centred * rstd
    normed = (normed_f * norm_gain + norm_shift).astype(jnp.bfloat16).reshape(-1, width)
    pre = jnp.dot(normed, expand, preferred_element_type=jnp.float32) + expandbias
    cdf = 0.5 * (1.0 + lax.erf(pre * 0.7071067811865476))
    act = (pre * cdf).astype(jnp.bfloat16)
    out_branch = jnp.dot(act, project, preferred_element_type=jnp.float32) + projectbias
    row_cells = lax.axis_index("rows") * height + jnp.arange(height, dtype=jnp.int32)
    col_cells = lax.axis_index("cols") * breadth + jnp.arange(breadth, dtype=jnp.int32)
    row_pick = (
        row_cells[:, None] // 8 == jnp.arange(tile_valid.shape[0], dtype=jnp.int32)[None, :]
    ).astype(jnp.float32)
    col_pick = (
        col_cells[:, None] // 8 == jnp.arange(tile_valid.shape[1], dtype=jnp.int32)[None, :]
    ).astype(jnp.float32)
    row_tiles = jnp.dot(row_pick, tile_valid.astype(jnp.float32), precision=lax.Precision.HIGHEST)
    cells = lax.dot_general(
        row_tiles, col_pick, (((1,), (1,)), ((), ())), precision=lax.Precision.HIGHEST
    )
    masked = (upstream.astype(jnp.float32) * cells[:, :, None]).reshape(-1, width)
    branch_grad = (masked * layer_scale).astype(jnp.bfloat16)
    act_grad = lax.dot_general(
        branch_grad, project, (((1,), (1,)), ((), ())), preferred_element_type=jnp.float32
    )
    slope = cdf + pre * jnp.exp(-0.5 * pre * pre) * 0.3989422804014327
    pre_grad = (act_grad * slope).astype(jnp.bfloat16)
    normed_grad = lax.dot_general(
        pre_grad, expand, (((1,), (1,)), ((), ())), preferred_element_type=jnp.float32
    ).reshape(height, breadth, width)
    gained = normed_grad * norm_gain
    mixed_grad = (
        rstd
        * (
            gained
            - jnp.mean(gained, axis=-1, keepdims=True)
            - normed_f * jnp.mean(gained * normed_f, axis=-1, keepdims=True)
        )
    ).astype(jnp.bfloat16)
    factor = float(height * row_count * breadth * col_count) ** (-0.5)
    project_low, project_sent = over_cores(
        lax.dot_general(
            act, branch_grad, (((0,), (0,)), ((), ())), preferred_element_type=jnp.float32
        )
        * factor,
        False,
    )
    expand_high, expand_sent = over_cores(
        lax.dot_general(
            normed, pre_grad, (((0,), (0,)), ((), ())), preferred_element_type=jnp.float32
        )
        * factor,
        True,
    )
    mixed_grad, project_sent, expand_sent = lax.optimization_barrier(
        (mixed_grad, project_sent, expand_sent)
    )
    features_grad, tap_sums = halo_call(
        backward_kernel,
        features.shape,
        [
            jax.ShapeDtypeStruct(features.shape, jnp.bfloat16),
            jax.ShapeDtypeStruct((49, width), jnp.float32),
        ],
        [
            pltpu.VMEM(features.shape, jnp.float32),
            pltpu.VMEM((49, 8, LANES), jnp.float32),
        ],
        1,
        2,
    )(mixed_grad, taps[::-1], masked.reshape(height, breadth, width), padded)
    grad_f = mixed_grad.astype(jnp.float32)
    local_sums = (
        tap_sums,
        jnp.sum(grad_f, axis=(0, 1)),
        jnp.sum(normed_grad * normed_f, axis=(0, 1)),
        jnp.sum(normed_grad, axis=(0, 1)),
        jnp.sum(pre_grad.astype(jnp.float32), axis=0),
        jnp.sum(branch_grad.astype(jnp.float32), axis=0),
        jnp.sum(masked * out_branch, axis=0),
    )
    packed = jnp.concatenate([value.reshape(-1, width) for value in local_sums], axis=0)
    high, low = split_rows(row_count)
    row = lax.axis_index("rows")
    project_high, project_sent = pick(over_low(project_low, project_sent), 0, high, row // low)
    expand_low, expand_sent = pick(over_high(expand_high, expand_sent), 0, low, row % low)
    packed, project_sent, expand_sent = lax.optimization_barrier(
        (packed, project_sent, expand_sent)
    )
    packed = whole_sum(packed) * factor
    project_grad = over_high(project_high, project_sent)
    expand_grad = over_low(expand_low, expand_sent)
    hidden = expand.shape[1]
    depthwise_grad = packed[:49].reshape(7, 7, width)
    depthbias_grad = packed[49]
    gain_grad = packed[50]
    shift_grad = packed[51]
    expandbias_grad = packed[52 : 52 + hidden // width].reshape(hidden)
    projectbias_grad = packed[52 + hidden // width]
    scale_grad = packed[53 + hidden // width]
    return (
        features_grad,
        depthwise_grad,
        depthbias_grad,
        gain_grad,
        shift_grad,
        expand_grad,
        expandbias_grad,
        project_grad,
        projectbias_grad,
        scale_grad,
    )


def solution(mesh):
    return jax.shard_map(
        per_device,
        mesh=mesh,
        in_specs=(
            P(("groups", "rows"), "cols", None),
            P(("groups", "rows"), "cols", None),
            P("groups", None),
            P(),
            P(),
            P(),
            P(),
            P(),
            P(),
            P(),
            P(),
            P(),
        ),
        out_specs=(
            P(("groups", "rows"), "cols", None),
            P("groups", None, None),
            P("groups"),
            P("groups"),
            P("groups"),
            P(("groups", "rows", "cols"), None),
            P("groups"),
            P(("groups", "rows", "cols"), None),
            P("groups"),
            P("groups"),
        ),
        check_vma=False,
    )
```
